768 devices in a mesh: segment: 48 (over x, z_lo, core), tensor: 16 (over z_hi, y).
Axes of the slice: x: 4, y: 8, z: 12 (z_hi: 2, z_lo: 6; z = z_hi * 6 + z_lo), core: 2. Of those that a mesh axis runs over, the one named last changes fastest.
Arguments:
- down_terms: bfloat16 [16, 6144, 8192], P('tensor', 'segment'), may hold values from -1.5 to 1.5
- residual: bfloat16 [6144, 8192], P(('segment', 'tensor'))
- norm_gain: bfloat16 [48, 8192], P('segment'), may hold values from 0.25 to 1.75
- key_value_weight: bfloat16 [48, 8192, 2048], P('segment', None, 'tensor'), may hold values from -0.0625 to 0.0625
- step_powers: int32 [3, 48, 64, 16], P(None, 'segment', None, 'tensor'), may hold values from -12 to -6, as said below
- bit_logits: float32 [80, 3], replicated, may hold values from -2 to 2
- layer_counts: int32 [48], replicated, may hold values from 1 to 4, 80 in all
Outputs:
- stream: bfloat16 [6144, 8192], P(('segment', 'tensor'))
- key_values: bfloat16 [6144, 2048], P('segment', 'tensor')
The draws below stay inside these ranges and needn't reach their ends.
Inputs may be any that keep to these rules, and one draw needn't show every extreme that they name: `layer_counts`: the counts sum to 80 and the largest is exactly 4. `step_powers`: entries of the 2, 4 and 8 bit candidates (first index 0, 1, 2) lie in -8 to -6, -9 to -7 and -12 to -10.
All inputs are finite; a program needn't handle non-finite values.
Results may differ from the reference program's by a relative error of at most 0.018.
Values may be sent and summed in bfloat16 or wider, within the bound.
A program may use at most 32 MiB of HBM per device.

```python
import math
import jax
import jax.numpy as jnp
import numpy as np
from jax import lax

D = 8192
TOK = 128
QTILE = 128
MOST = 4
KV2 = 2048
LAYERS = 80
TOKENS = 6144
N_SEGMENT = 48
N_TENSOR = 16


def draw_residual(key, part):
    first_key, second_key = jax.random.split(key, 2)
    columns = 0.3 * jnp.exp(jax.random.uniform(first_key, (1, D), jnp.float32) * jnp.log(10.0))
    result = jax.random.normal(second_key, (TOKENS, D), jnp.float32) * columns
    return result.astype(jnp.bfloat16)


def draw_step_powers(key, part):
    bases = jnp.array([-8, -9, -12], jnp.int32).reshape(3, 1, 1, 1)
    offsets = jax.random.randint(key, (3, N_SEGMENT, D // QTILE, KV2 // QTILE), 0, 3, jnp.int32)
    return bases + offsets


def block_scale(stream_key, dims, cuts, smallest, high):
    level = 1.0
    for axis_at, shards_of in cuts:
        draws = jax.random.uniform(jax.random.fold_in(jax.random.fold_in(stream_key, 6), axis_at), (shards_of,), jnp.float32, smallest / len(cuts), high / len(cuts))
        level = level * jnp.repeat(jnp.exp(draws), dims[axis_at] // shards_of).reshape((-1,) + (1,) * (len(dims) - 1 - axis_at))
    return level


def split_up(count, total, limit, slope):
    loads = [(1 << 20) // math.isqrt(rank ** slope) + 1 for rank in range(2, count + 1)]
    spare, counts = total - limit - (count - 1), [1] * (count - 1)
    while spare > 0:
        candidates = [i for i in range(count - 1) if counts[i] < limit]
        mass, left = sum([loads[i] for i in candidates]), spare
        for i in candidates:
            addition = min(limit - counts[i], max(1, left * loads[i] // mass), spare)
            counts[i] = counts[i] + addition
            spare = spare - addition
    return np.array([limit] + counts)


def ragged(rng, amount, total, limit, lean):
    if amount == 2:
        one = jax.random.randint(rng, (), max(1, total - limit), min(limit, total - 1) + 1)
        return jnp.stack([one, total - one])
    tallies = jnp.asarray(split_up(amount, total, limit, lean), jnp.int32)
    pairs = (amount - 1) // 2
    source_of, taker = tallies[1:1 + 2 * pairs:2], tallies[2:2 + 2 * pairs:2]
    slack = jnp.minimum(source_of - 1, limit - taker)
    shifted = jax.random.randint(jax.random.fold_in(rng, 1), (pairs,), 0, 1 << 20) % (slack + 1)
    tallies = tallies.at[1:1 + 2 * pairs:2].set(source_of - shifted).at[2:2 + 2 * pairs:2].set(taker + shifted)
    return tallies[jax.random.permutation(jax.random.fold_in(rng, 2), amount)]


def gaussian(own_key, dims, deviation, most, cuts=(), dtype=jnp.bfloat16):
    entries = jax.random.normal(own_key, dims, jnp.float32) * deviation
    if len(cuts) > 0:
        entries = block_scale(own_key, dims, cuts, -0.22, 0.18) * entries
    return jnp.clip(entries, min=-most, max=most).astype(dtype)


def setup_inputs(seed: int = 0) -> dict:
    streams_of = jax.random.split(jax.random.key(seed), 8)
    down_terms = gaussian(streams_of[0], (N_TENSOR, TOKENS, D), 0.25, 1.5, ((0, 16), (1, 48)))
    residual = draw_residual(jax.random.fold_in(streams_of[7], 71), 0)
    norm_gain = jnp.clip(1.0 + 0.15 * jax.random.normal(streams_of[2], (N_SEGMENT, D), jnp.float32), 0.25, 1.75).astype(jnp.bfloat16)
    key_value_weight = gaussian(streams_of[3], (N_SEGMENT, D, KV2), D ** -0.5, 0.0625, ((0, 48), (2, 16)))
    step_powers = draw_step_powers(jax.random.fold_in(streams_of[7], 71), 0)
    bit_logits = jnp.clip(jax.random.uniform(streams_of[5], (LAYERS, 3), jnp.float32, -2.0, 2.0), -2.0, 2.0)
    layer_counts = ragged(streams_of[6], N_SEGMENT, LAYERS, MOST, 2).astype(jnp.int32)
    return dict(down_terms=down_terms, residual=residual, norm_gain=norm_gain, key_value_weight=key_value_weight, step_powers=step_powers, bit_logits=bit_logits, layer_counts=layer_counts)


def step_sizes(powers):
    sizes = jnp.zeros(powers.shape, jnp.float32)
    for power in range(-12, -5):
        sizes = jnp.where(powers == power, 2.0 ** power, sizes)
    return sizes

def mix_weight(weight, powers, shares, tile):
    height, width = weight.shape
    values = weight.astype(jnp.float32).reshape(height // tile, tile, width // tile, tile)
    total = jnp.zeros_like(values)
    for which, bits in enumerate((2, 4, 8)):
        step = step_sizes(powers[which])[:, None, :, None]
        levels = jnp.clip(jnp.floor(values / step + 0.5), -2.0 ** (bits - 1), 2.0 ** (bits - 1) - 1.0)
        total = total + shares[which] * (levels * step)
    return total.reshape(height, width).astype(jnp.bfloat16)

def rms_scale(stream, gain):
    values = stream.astype(jnp.float32)
    mean_square = lax.optimization_barrier(jnp.mean(values * values, axis=-1, keepdims=True))
    return (values * lax.rsqrt(mean_square + 1e-05) * gain.astype(jnp.float32)).astype(jnp.bfloat16)

def reference(down_terms, residual, norm_gain, key_value_weight, step_powers, bit_logits, layer_counts):

    def add_term(total, term):
        return (total + term.astype(jnp.float32), None)
    summed, unused = lax.scan(add_term, jnp.zeros((TOKENS, D), jnp.float32), down_terms)
    hidden = (summed + residual.astype(jnp.float32)).astype(jnp.bfloat16)
    arrived = jnp.roll(hidden.reshape(N_SEGMENT, TOK, D), 1, axis=0)
    starts = (jnp.cumsum(layer_counts) - layer_counts).astype(jnp.int32)

    def section(items):
        rows, gain, weight, powers, first = items
        raised = jnp.exp(bit_logits[first])
        shares = raised / jnp.sum(raised)
        mixed = mix_weight(weight, powers, shares, QTILE)
        normed = rms_scale(rows, gain)
        return jnp.dot(normed, mixed, preferred_element_type=jnp.float32).astype(jnp.bfloat16)
    outputs = lax.map(section, (arrived, norm_gain, key_value_weight, jnp.moveaxis(step_powers, 1, 0), starts))
    return (arrived.reshape(TOKENS, D), outputs.reshape(TOKENS, KV2))
```

```python
import jax
import jax.numpy as jnp
from jax import lax
from jax.experimental import pallas as pl
from jax.experimental.pallas import tpu as pltpu
from jax.sharding import PartitionSpec as P

MESH = pl.DeviceIdType.MESH
QTILE = 128
RING = 8
CHUNKS = 8
BLOCK = 16
LIMIT = 1e30
BITS = (2, 4, 8)
LOWEST = (-8, -9, -12)


def hops(direction, chunk):
    return 4 if (chunk + direction) % 2 == 0 else 3


def schedule(chunks, stagger=0.6, step=1.0, cross=4.0):
    steps = []
    for c in range(chunks):
        begin = stagger * c
        for s in range(1, 5):
            steps.append((begin + step * (s - 1), 0, ("reduce", c, s)))
        done = begin + step * 4
        steps.append((done, 0, ("finish", c, 0)))
        steps.append((done + cross, 1, ("hidden", c, 0)))
        for s in range(1, 4):
            steps.append((done + cross + step * s, 1, ("gather", c, s)))
        steps.append((done + cross + step * 4.5, 2, ("product", c, 0)))
        steps.append((1.5 + 0.7 * c, 3, ("mix", c, 0)))
    steps.sort(key=lambda item: item[:2])
    return [item[2] for item in steps]


def kernel(
    powers, logits, counts, terms_hbm, residual_hbm, gain, weight_hbm,
    stream, key_values,
    terms, residual, weight, mixed, arrived, partial, crossed, gathered, scaled, total, squares,
    load_sem, reduce_send, reduce_recv, cross_send, cross_recv, gather_send, gather_recv,
):
    f32, bf16 = jnp.float32, jnp.bfloat16
    section, sections = lax.axis_index("segment"), lax.axis_size("segment")
    t = lax.axis_index("tensor")
    y, z = lax.rem(t, RING), lax.div(t, RING)
    ring = z * RING
    neighbour = (ring + lax.rem(y + 1, RING), ring + lax.rem(y + RING - 1, RING))
    far = lax.rem(t + RING, 2 * RING)
    after, before = lax.rem(section + 1, sections), lax.rem(section + sections - 1, sections)
    depth = terms.shape[1]
    width = depth // CHUNKS

    def columns(c):
        return pl.ds(c * width, width)

    def rows(d):
        return pl.ds(pl.multiple_of(lax.rem(d + 2 * RING, RING) * BLOCK, BLOCK), BLOCK)

    def offset(direction, distance):
        return y + distance if direction == 0 else y - distance

    loads = [
        pltpu.make_async_copy(residual_hbm, residual, load_sem.at[0]),
        pltpu.make_async_copy(terms_hbm, terms, load_sem.at[1]),
        pltpu.make_async_copy(weight_hbm, weight, load_sem.at[2]),
    ]
    for load in loads:
        load.start()

    barrier = pltpu.get_barrier_semaphore()
    for there in (neighbour[0], neighbour[1]):
        pl.semaphore_signal(barrier, inc=1, device_id=(section, there), device_id_type=MESH)
    for there in (t, far):
        pl.semaphore_signal(barrier, inc=1, device_id=(before, there), device_id_type=MESH)

    first = jnp.int32(0)
    for q in range(sections):
        first = first + jnp.where(q < section, counts[q], 0)
    raised = [jnp.exp(jnp.full((8, 128), logits[first, b], f32)) for b in range(3)]
    whole = raised[0] + raised[1] + raised[2]
    shares = [(r / whole)[0:1, :] for r in raised]

    loads[0].wait()
    loads[1].wait()
    own = pl.ds(pl.multiple_of(lax.div(t, 2) * BLOCK, BLOCK), BLOCK)
    half = lax.rem(t, 2)
    row = lax.broadcasted_iota(jnp.int32, (BLOCK, width), 0)
    mine = lax.div(row, 8) == half
    for c in range(CHUNKS):
        extra = residual[:, columns(c)].astype(f32)
        extra = jnp.where(mine, jnp.concatenate([extra, extra], axis=0), 0.0)
        terms[own, columns(c)] = (terms[own, columns(c)].astype(f32) + extra).astype(bf16)

    pl.semaphore_wait(barrier, 4)

    sent = []

    def send(src, dst, send_sem, recv_sem, there):
        copy = pltpu.make_async_remote_copy(
            src_ref=src, dst_ref=dst, send_sem=send_sem, recv_sem=recv_sem,
            device_id=there, device_id_type=MESH,
        )
        copy.start()
        sent.append(copy)

    def receive(dst, recv_sem):
        pltpu.make_async_remote_copy(
            src_ref=dst, dst_ref=dst, send_sem=recv_sem, recv_sem=recv_sem,
            device_id=(section, neighbour[0]), device_id_type=MESH,
        ).wait_recv()

    def reduce(c, s):
        for direction in range(2):
            length = hops(direction, c)
            if s > length:
                continue
            d = rows(offset(direction, length + 1 - s))
            if s == 1:
                src = terms.at[d, columns(c)]
            else:
                src = arrived.at[direction, s - 2, :, columns(c)]
                receive(src, reduce_recv.at[direction, s - 2, c])
                src[...] = (src[...].astype(f32) + terms[d, columns(c)].astype(f32)).astype(bf16)
            send(
                src,
                arrived.at[direction, s - 1, :, columns(c)],
                reduce_send.at[direction, s - 1, c],
                reduce_recv.at[direction, s - 1, c],
                (section, neighbour[direction]),
            )

    def finish(c, s):
        value = terms[rows(y), columns(c)].astype(f32)
        for direction in (1, 0) if hops(0, c) == 4 else (0, 1):
            last = hops(direction, c) - 1
            src = arrived.at[direction, last, :, columns(c)]
            receive(src, reduce_recv.at[direction, last, c])
            value = value + src[...].astype(f32)
        partial[:, columns(c)] = value.astype(bf16)
        for slot, there in ((1, far), (0, t)):
            send(
                partial.at[:, columns(c)],
                crossed.at[slot, :, columns(c)],
                cross_send.at[slot, c],
                cross_recv.at[slot, c],
                (after, there),
            )

    def pass_on(c, s, d):
        for direction in range(2):
            if s > hops(direction, c):
                continue
            block = gathered.at[rows(offset(direction, -(s - 1))), columns(c)]
            if s > 1:
                receive(block, gather_recv.at[direction, s - 2, c])
            send(
                block, block, gather_send.at[direction, s - 1, c], gather_recv.at[direction, s - 1, c],
                (section, neighbour[direction]),
            )

    def hidden(c, s):
        for slot in range(2):
            receive(crossed.at[slot, :, columns(c)], cross_recv.at[slot, c])
        value = crossed[0, :, columns(c)].astype(f32) + crossed[1, :, columns(c)].astype(f32)
        gathered[rows(y), columns(c)] = value.astype(bf16)
        pass_on(c, 1, None)

    def gather(c, s):
        pass_on(c, s + 1, None)

    def product(c, s):
        for direction in range(2):
            last = hops(direction, c)
            block = gathered.at[rows(offset(direction, -last)), columns(c)]
            receive(block, gather_recv.at[direction, last - 1, c])
        piece = 256
        for j in range(width // piece):
            at = pl.ds(c * width + j * piece, piece)
            values = gathered[:, at].astype(f32)
            square = values * values
            square = square[:, :128] + square[:, 128:]
            if c == first_product and j == 0:
                squares[...] = square
            else:
                squares[...] += square
            values = jnp.clip(values * gain[0:1, at].astype(f32), -LIMIT, LIMIT)
            scaled[:, pl.ds(j * piece, piece)] = values.astype(bf16)
        result = jnp.dot(scaled[...], mixed[columns(c), :], preferred_element_type=f32)
        if c == first_product:
            total[...] = result
        else:
            total[...] += result
        block = gathered[own, columns(c)].astype(f32)
        stream[:, columns(c)] = jnp.where(half == 0, block[:8], block[8:]).astype(bf16)

    def mix(c, s):
        if c == 0:
            loads[2].wait()
        tiles = width // QTILE

        def one(i, carry):
            tile = c * tiles + i
            at = pl.ds(pl.multiple_of(tile * QTILE, QTILE), QTILE)
            values = weight[at, :].astype(f32)
            result = None
            for b, bits in enumerate(BITS):
                power, low = powers[b * (depth // QTILE) + tile], LOWEST[b]
                step = jnp.where(power == low, 2.0**low, jnp.where(power == low + 1, 2.0 ** (low + 1), 2.0 ** (low + 2)))
                inverse = jnp.where(power == low, 2.0**-low, jnp.where(power == low + 1, 2.0 ** (-low - 1), 2.0 ** (-low - 2)))
                levels = jnp.clip(jnp.floor(values * inverse + 0.5), -(2.0 ** (bits - 1)), 2.0 ** (bits - 1) - 1.0)
                part = levels * (shares[b] * step)
                result = part if result is None else result + part
            mixed[at, :] = result.astype(bf16)
            return carry

        lax.fori_loop(0, tiles, one, 0)

    order = schedule(CHUNKS)
    first_product = [c for name, c, s in order if name == "product"][0]
    act = dict(reduce=reduce, finish=finish, hidden=hidden, gather=gather, product=product, mix=mix)
    for name, c, s in order:
        act[name](c, s)

    mean = jnp.sum(squares[...], axis=1, keepdims=True) * (1.0 / depth)
    key_values[...] = (total[...] * lax.rsqrt(mean + 1e-05)).astype(bf16)
    for copy in sent:
        copy.wait_send()


def body(down_terms, residual, norm_gain, key_value_weight, step_powers, bit_logits, layer_counts):
    terms, weight = down_terms[0], key_value_weight[0]
    depth, wide = weight.shape
    bf16, f32 = jnp.bfloat16, jnp.float32
    vmem, smem, anywhere = pltpu.VMEM, pltpu.SMEM, pl.ANY
    dma = pltpu.SemaphoreType.DMA
    return pl.pallas_call(
        kernel,
        out_shape=(
            jax.ShapeDtypeStruct(residual.shape, bf16),
            jax.ShapeDtypeStruct((terms.shape[0], wide), bf16),
        ),
        in_specs=[
            pl.BlockSpec(memory_space=smem),
            pl.BlockSpec(memory_space=smem),
            pl.BlockSpec(memory_space=smem),
            pl.BlockSpec(memory_space=anywhere),
            pl.BlockSpec(memory_space=anywhere),
            pl.BlockSpec(memory_space=vmem),
            pl.BlockSpec(memory_space=anywhere),
        ],
        out_specs=(pl.BlockSpec(memory_space=vmem), pl.BlockSpec(memory_space=vmem)),
        scratch_shapes=[
            vmem(terms.shape, bf16),
            vmem(residual.shape, bf16),
            vmem(weight.shape, bf16),
            vmem(weight.shape, bf16),
            vmem((2, 4, BLOCK, depth), bf16),
            vmem((BLOCK, depth), bf16),
            vmem((2, BLOCK, depth), bf16),
            vmem(terms.shape, bf16),
            vmem((terms.shape[0], depth // CHUNKS), bf16),
            vmem((terms.shape[0], wide), f32),
            vmem((terms.shape[0], 128), f32),
            dma((3,)),
            dma((2, 4, CHUNKS)),
            dma((2, 4, CHUNKS)),
            dma((2, CHUNKS)),
            dma((2, CHUNKS)),
            dma((2, 4, CHUNKS)),
            dma((2, 4, CHUNKS)),
        ],
        compiler_params=pltpu.CompilerParams(
            collective_id=0, has_side_effects=True, vmem_limit_bytes=56 << 20
        ),
    )(
        step_powers.reshape(-1), bit_logits, layer_counts, terms, residual, norm_gain, weight,
    )


def solution(mesh):
    return jax.shard_map(
        body,
        mesh=mesh,
        in_specs=(
            P("tensor", "segment", None),
            P(("segment", "tensor"), None),
            P("segment", None),
            P("segment", None, "tensor"),
            P(None, "segment", None, "tensor"),
            P(),
            P(),
        ),
        out_specs=(P(("segment", "tensor"), None), P("segment", "tensor")),
        check_vma=False,
    )
```

```python
import jax
import jax.numpy as jnp
from jax import lax
from jax.experimental import pallas as pl
from jax.experimental.pallas import tpu as pltpu
from jax.sharding import PartitionSpec as P

MESH = pl.DeviceIdType.MESH
QTILE = 128
RING = 8
SIZES = (2048,) * 4
CHUNKS = len(SIZES)
STAGGER, STEP, CROSS = 0.6, 1.0, 4.0
BLOCK = 16
LIMIT = 1e30
FIRST = 3
BITS = (2, 4, 8)
LOWEST = (-8, -9, -12)


def hops(direction, chunk):
    return 4 if (chunk + direction) % 2 == 0 else 3


def schedule(chunks, stagger=STAGGER, step=STEP, cross=CROSS):
    steps = []
    for c in range(chunks):
        begin = stagger * c
        for s in range(1, 5):
            steps.append((begin + step * (s - 1), 0, ("reduce", c, s)))
        done = begin + step * 4
        steps.append((done, 0, ("finish", c, 0)))
        steps.append((done + cross, 1, ("hidden", c, 0)))
        for s in range(1, 4):
            steps.append((done + cross + step * s, 1, ("gather", c, s)))
        steps.append((done + cross + step * 4.5, 2, ("product", c, 0)))
        steps.append((1.5 + 0.7 * c, 3, ("mix", c, 0)))
    steps.sort(key=lambda item: item[:2])
    return [item[2] for item in steps]


def kernel(
    powers_hbm, logits_hbm, counts_hbm, terms_hbm, residual_hbm, gain_hbm, weight_hbm,
    stream, key_values,
    powers, logits, counts, gain, taken, product_out,
    terms, residual, weight, mixed, arrived, partial, crossed, gathered, scaled, total, squares,
    load_sem, term_sem, store_sem, reduce_send, reduce_recv, cross_send, cross_recv, gather_send, gather_recv,
):
    f32, bf16 = jnp.float32, jnp.bfloat16
    section, sections = lax.axis_index("segment"), lax.axis_size("segment")
    t = lax.axis_index("tensor")
    y, z = lax.rem(t, RING), lax.div(t, RING)
    ring = z * RING
    neighbour = (ring + lax.rem(y + 1, RING), ring + lax.rem(y + RING - 1, RING))
    far = lax.rem(t + RING, 2 * RING)
    after, before = lax.rem(section + 1, sections), lax.rem(section + sections - 1, sections)
    depth = terms.shape[1]
    starts = [sum(SIZES[:c]) for c in range(CHUNKS)]

    def columns(c):
        return pl.ds(starts[c], SIZES[c])

    def rows(d):
        return pl.ds(pl.multiple_of(lax.rem(d + 2 * RING, RING) * BLOCK, BLOCK), BLOCK)

    def offset(direction, distance):
        return y + distance if direction == 0 else y - distance

    barrier = pltpu.get_barrier_semaphore()
    for there in (neighbour[0], neighbour[1]):
        pl.semaphore_signal(barrier, inc=1, device_id=(section, there), device_id_type=MESH)
    for there in (t, far):
        pl.semaphore_signal(barrier, inc=1, device_id=(before, there), device_id_type=MESH)

    loads = [
        pltpu.make_async_copy(src, dst, load_sem.at[i])
        for i, (src, dst) in enumerate((
            (residual_hbm, residual), (counts_hbm, counts), (logits_hbm, logits),
            (powers_hbm, powers), (weight_hbm, weight), (gain_hbm, gain),
        ))
    ]
    term_loads = [
        pltpu.make_async_copy(terms_hbm.at[:, columns(c)], terms.at[:, columns(c)], term_sem.at[c])
        for c in range(CHUNKS)
    ]
    loads[0].start()
    for load in term_loads + loads[1:]:
        load.start()

    loads[0].wait()
    own = pl.ds(pl.multiple_of(lax.div(t, 2) * BLOCK, BLOCK), BLOCK)
    half = lax.rem(t, 2)

    def join(c, s):
        term_loads[c].wait()
        extra = residual[:, columns(c)].astype(f32)
        mine = lax.div(lax.broadcasted_iota(jnp.int32, (BLOCK, SIZES[c]), 0), 8) == half
        extra = jnp.where(mine, jnp.concatenate([extra, extra], axis=0), 0.0)
        terms[own, columns(c)] = (terms[own, columns(c)].astype(f32) + extra).astype(bf16)

    sent, stores = [], []

    def send(src, dst, send_sem, recv_sem, there):
        copy = pltpu.make_async_remote_copy(
            src_ref=src, dst_ref=dst, send_sem=send_sem, recv_sem=recv_sem,
            device_id=there, device_id_type=MESH,
        )
        copy.start()
        sent.append(copy)

    def receive(dst, recv_sem):
        pltpu.make_async_remote_copy(
            src_ref=dst, dst_ref=dst, send_sem=recv_sem, recv_sem=recv_sem,
            device_id=(section, neighbour[0]), device_id_type=MESH,
        ).wait_recv()

    def reduce(c, s):
        for direction in range(2):
            length = hops(direction, c)
            if s > length:
                continue
            d = rows(offset(direction, length + 1 - s))
            if s == 1:
                src = terms.at[d, columns(c)]
            else:
                src = arrived.at[direction, s - 2, :, columns(c)]
                receive(src, reduce_recv.at[direction, s - 2, c])
                src[...] = (src[...].astype(f32) + terms[d, columns(c)].astype(f32)).astype(bf16)
            send(
                src,
                arrived.at[direction, s - 1, :, columns(c)],
                reduce_send.at[direction, s - 1, c],
                reduce_recv.at[direction, s - 1, c],
                (section, neighbour[direction]),
            )

    def finish(c, s):
        value = terms[rows(y), columns(c)].astype(f32)
        for direction in (1, 0) if hops(0, c) == 4 else (0, 1):
            last = hops(direction, c) - 1
            src = arrived.at[direction, last, :, columns(c)]
            receive(src, reduce_recv.at[direction, last, c])
            value = value + src[...].astype(f32)
        partial[:, columns(c)] = value.astype(bf16)
        for slot, there in ((1, far), (0, t)):
            send(
                partial.at[:, columns(c)],
                crossed.at[slot, :, columns(c)],
                cross_send.at[slot, c],
                cross_recv.at[slot, c],
                (after, there),
            )

    def pass_on(c, s, d):
        for direction in range(2):
            if s > hops(direction, c):
                continue
            block = gathered.at[rows(offset(direction, -(s - 1))), columns(c)]
            if s > 1:
                receive(block, gather_recv.at[direction, s - 2, c])
            send(
                block, block, gather_send.at[direction, s - 1, c], gather_recv.at[direction, s - 1, c],
                (section, neighbour[direction]),
            )

    def hidden(c, s):
        for slot in range(2):
            receive(crossed.at[slot, :, columns(c)], cross_recv.at[slot, c])
        value = crossed[0, :, columns(c)].astype(f32) + crossed[1, :, columns(c)].astype(f32)
        gathered[rows(y), columns(c)] = value.astype(bf16)
        pass_on(c, 1, None)

    def gather(c, s):
        pass_on(c, s + 1, None)

    def product(c, s):
        for direction in range(2):
            last = hops(direction, c)
            block = gathered.at[rows(offset(direction, -last)), columns(c)]
            receive(block, gather_recv.at[direction, last - 1, c])
        piece = 256
        for j in range(SIZES[c] // piece):
            at = pl.ds(starts[c] + j * piece, piece)
            values = gathered[:, at].astype(f32)
            square = values * values
            square = square[:, :128] + square[:, 128:]
            if c == first_product and j == 0:
                squares[...] = square
            else:
                squares[...] += square
            values = jnp.clip(values * gain[0:1, at].astype(f32), -LIMIT, LIMIT)
            scaled[:, pl.ds(j * piece, piece)] = values.astype(bf16)
        result = jnp.dot(scaled[:, : SIZES[c]], mixed[columns(c), :], preferred_element_type=f32)
        if c == first_product:
            total[...] = result
        else:
            total[...] += result
        block = gathered[own, columns(c)].astype(f32)
        taken[:, columns(c)] = jnp.where(half == 0, block[:8], block[8:]).astype(bf16)
        stores.append(pltpu.make_async_copy(taken.at[:, columns(c)], stream.at[:, columns(c)], store_sem.at[c]))
        stores[-1].start()

    def mix(c, s):
        tiles = SIZES[c] // QTILE

        def one(i, carry):
            tile = starts[c] // QTILE + i
            at = pl.ds(pl.multiple_of(tile * QTILE, QTILE), QTILE)
            values = weight[at, :].astype(f32)
            result = None
            for b, bits in enumerate(BITS):
                power, low = powers[b, 0, 0, tile], LOWEST[b]
                step = jnp.where(power == low, 2.0**low, jnp.where(power == low + 1, 2.0 ** (low + 1), 2.0 ** (low + 2)))
                inverse = jnp.where(power == low, 2.0**-low, jnp.where(power == low + 1, 2.0 ** (-low - 1), 2.0 ** (-low - 2)))
                levels = jnp.clip(jnp.floor(values * inverse + 0.5), -(2.0 ** (bits - 1)), 2.0 ** (bits - 1) - 1.0)
                part = levels * (shares[b] * step)
                result = part if result is None else result + part
            mixed[at, :] = result.astype(bf16)
            return carry

        lax.fori_loop(0, tiles, one, 0)

    join(0, 0)
    pl.semaphore_wait(barrier, 4)
    reduce(0, 1)
    for c in range(1, CHUNKS):
        join(c, 0)
        if c < FIRST:
            reduce(c, 1)
    for load in loads[1:]:
        load.wait()
    first = jnp.int32(0)
    for q in range(sections):
        first = first + jnp.where(q < section, counts[q], 0)
    raised = [jnp.exp(jnp.full((8, 128), logits[b, first], f32)) for b in range(3)]
    whole = raised[0] + raised[1] + raised[2]
    shares = [(r / whole)[0:1, :] for r in raised]

    order = [x for x in schedule(CHUNKS) if x[0] != "reduce" or x[2] > 1 or x[1] >= FIRST]
    first_product = [c for name, c, s in order if name == "product"][0]
    act = dict(reduce=reduce, finish=finish, hidden=hidden, gather=gather, product=product, mix=mix)
    for name, c, s in order:
        act[name](c, s)

    mean = jnp.sum(squares[...], axis=1, keepdims=True) * (1.0 / depth)
    product_out[...] = (total[...] * lax.rsqrt(mean + 1e-05)).astype(bf16)
    stores.append(pltpu.make_async_copy(product_out, key_values, store_sem.at[CHUNKS]))
    stores[-1].start()
    for copy in sent:
        copy.wait_send()
    for copy in stores:
        copy.wait()


def hand_out(stream_in, product_in, stream, key_values):
    stream[...] = stream_in[...]
    key_values[...] = product_in[...]


def body(down_terms, residual, norm_gain, key_value_weight, step_powers, bit_logits, layer_counts):
    terms, weight = down_terms[0], key_value_weight[0]
    depth, wide = weight.shape
    bf16, f32 = jnp.bfloat16, jnp.float32
    vmem, smem, anywhere = pltpu.VMEM, pltpu.SMEM, pl.ANY
    dma = pltpu.SemaphoreType.DMA
    out_shape = (
        jax.ShapeDtypeStruct(residual.shape, bf16),
        jax.ShapeDtypeStruct((terms.shape[0], wide), bf16),
    )
    powers = jnp.swapaxes(step_powers, 2, 3)
    logits = bit_logits.T
    outs = pl.pallas_call(
        kernel,
        out_shape=out_shape,
        in_specs=[pl.BlockSpec(memory_space=anywhere)] * 7,
        out_specs=(pl.BlockSpec(memory_space=anywhere),) * 2,
        scratch_shapes=[
            smem(powers.shape, jnp.int32),
            smem(logits.shape, f32),
            smem(layer_counts.shape, jnp.int32),
            vmem(norm_gain.shape, bf16),
            vmem(residual.shape, bf16),
            vmem((terms.shape[0], wide), bf16),
            vmem(terms.shape, bf16),
            vmem(residual.shape, bf16),
            vmem(weight.shape, bf16),
            vmem(weight.shape, bf16),
            vmem((2, 4, BLOCK, depth), bf16),
            vmem((BLOCK, depth), bf16),
            vmem((2, BLOCK, depth), bf16),
            vmem(terms.shape, bf16),
            vmem((terms.shape[0], max(SIZES)), bf16),
            vmem((terms.shape[0], wide), f32),
            vmem((terms.shape[0], 128), f32),
            dma((6,)),
            dma((CHUNKS,)),
            dma((CHUNKS + 1,)),
            dma((2, 4, CHUNKS)),
            dma((2, 4, CHUNKS)),
            dma((2, CHUNKS)),
            dma((2, CHUNKS)),
            dma((2, 4, CHUNKS)),
            dma((2, 4, CHUNKS)),
        ],
        compiler_params=pltpu.CompilerParams(
            collective_id=0, has_side_effects=True, vmem_limit_bytes=56 << 20
        ),
    )(powers, logits, layer_counts, terms, residual, norm_gain, weight)
    return pl.pallas_call(
        hand_out,
        out_shape=out_shape,
        in_specs=[pl.BlockSpec(memory_space=vmem)] * 2,
        out_specs=(pl.BlockSpec(memory_space=vmem),) * 2,
        compiler_params=pltpu.CompilerParams(vmem_limit_bytes=56 << 20),
    )(*outs)


def solution(mesh):
    return jax.shard_map(
        body,
        mesh=mesh,
        in_specs=(
            P("tensor", "segment", None),
            P(("segment", "tensor"), None),
            P("segment", None),
            P("segment", None, "tensor"),
            P(None, "segment", None, "tensor"),
            P(),
            P(),
        ),
        out_specs=(P(("segment", "tensor"), None), P("segment", "tensor")),
        check_vma=False,
    )
```

```python
import jax
import jax.numpy as jnp
from jax import lax
from jax.experimental import pallas as pl
from jax.experimental.pallas import tpu as pltpu
from jax.sharding import PartitionSpec as P

MESH = pl.DeviceIdType.MESH
QTILE = 128
RING = 8
SIZES = (2048,) * 4
CHUNKS = len(SIZES)
STAGGER, STEP, CROSS, SPREAD = 0.6, 1.0, 4.0, 0.6
BLOCK = 16
LIMIT = 1e30
RELAY = 1.6
FIRST = 3
RELAYED = (0,)
RUN = 12
BITS = (2, 4, 8)
LOWEST = (-8, -9, -12)


def hops(direction, chunk):
    return 4 if (chunk + direction) % 2 == 0 else 3


def schedule(chunks, stagger=STAGGER, step=STEP, cross=CROSS):
    steps = []
    for c in range(chunks):
        begin = stagger * c
        for s in range(1, 5):
            steps.append((begin + step * (s - 1), 0, ("reduce", c, s)))
        done = begin + step * 4
        ready = step * 4 + cross + SPREAD * c
        steps.append((done, 0, ("finish", c, 0)))
        steps.append((ready, 1, ("hidden", c, 0)))
        if c in RELAYED:
            steps.append((done + RELAY, 0, ("relay", c, 0)))
        for s in range(1, 4):
            steps.append((ready + step * s, 1, ("gather", c, s)))
        steps.append((ready + step * 4.5, 2, ("product", c, 0)))
        steps.append((1.5 + 0.7 * c, 3, ("mix", c, 0)))
    steps.sort(key=lambda item: item[:2])
    return [item[2] for item in steps]


def kernel(
    powers_hbm, logits_hbm, counts_hbm, terms_hbm, residual_hbm, gain_hbm, weight_hbm,
    stream, key_values,
    powers, logits, counts, gain, taken, product_out,
    terms, residual, weight, mixed, arrived, partial, crossed, gathered, scaled, total, squares,
    load_sem, term_sem, store_sem, reduce_send, reduce_recv, cross_send, cross_recv, gather_send, gather_recv,
    relayed, relay_send, relay_recv,
):
    f32, bf16 = jnp.float32, jnp.bfloat16
    section, sections = lax.axis_index("segment"), lax.axis_size("segment")
    t = lax.axis_index("tensor")
    y, z = lax.rem(t, RING), lax.div(t, RING)
    ring = z * RING
    neighbour = (ring + lax.rem(y + 1, RING), ring + lax.rem(y + RING - 1, RING))
    far = lax.rem(t + RING, 2 * RING)
    after, before = lax.rem(section + 1, sections), lax.rem(section + sections - 1, sections)
    place = lax.rem(section, RUN)
    spot = lax.div(place, 2)
    first_core = lax.rem(place, 2) == 0
    by_relay = jnp.logical_and(lax.rem(spot, 2) == 1, first_core)
    is_relay = jnp.logical_and(lax.rem(spot, 2) == 0, first_core)
    last_spot = RUN // 2 - 1
    wrapped = lax.div(spot, last_spot)
    relay_at = (section - place + lax.rem(place + 2, RUN), lax.rem(t + RING * wrapped, 2 * RING))
    wraps = lax.div(last_spot - spot, last_spot)
    relay_source = (section - place + lax.rem(place + RUN - 2, RUN), lax.rem(t + RING * wraps, 2 * RING))
    relay_target = (section - place + lax.rem(place + RUN - 1, RUN), lax.rem(t + RING + RING * wraps, 2 * RING))
    is_target = jnp.logical_and(lax.rem(spot, 2) == 1, lax.rem(place, 2) == 1)
    relay_from = (section - place + lax.rem(place + 1, RUN), lax.rem(t + RING + RING * wrapped, 2 * RING))

    depth = terms.shape[1]
    starts = [sum(SIZES[:c]) for c in range(CHUNKS)]

    def columns(c):
        return pl.ds(starts[c], SIZES[c])

    def rows(d):
        return pl.ds(pl.multiple_of(lax.rem(d + 2 * RING, RING) * BLOCK, BLOCK), BLOCK)

    def offset(direction, distance):
        return y + distance if direction == 0 else y - distance

    barrier = pltpu.get_barrier_semaphore()
    for there in (neighbour[0], neighbour[1]):
        pl.semaphore_signal(barrier, inc=1, device_id=(section, there), device_id_type=MESH)
    for there in (t, far):
        pl.semaphore_signal(barrier, inc=1, device_id=(before, there), device_id_type=MESH)

    @pl.when(is_relay)
    def _():
        pl.semaphore_signal(barrier, inc=1, device_id=relay_source, device_id_type=MESH)

    @pl.when(is_target)
    def _():
        pl.semaphore_signal(barrier, inc=1, device_id=relay_from, device_id_type=MESH)

    loads = [
        pltpu.make_async_copy(src, dst, load_sem.at[i])
        for i, (src, dst) in enumerate((
            (residual_hbm, residual), (counts_hbm, counts), (logits_hbm, logits),
            (powers_hbm, powers), (weight_hbm, weight), (gain_hbm, gain),
        ))
    ]
    term_loads = [
        pltpu.make_async_copy(terms_hbm.at[:, columns(c)], terms.at[:, columns(c)], term_sem.at[c])
        for c in range(CHUNKS)
    ]
    loads[0].start()
    for load in term_loads + loads[1:]:
        load.start()

    loads[0].wait()
    own = pl.ds(pl.multiple_of(lax.div(t, 2) * BLOCK, BLOCK), BLOCK)
    half = lax.rem(t, 2)

    def join(c, s):
        term_loads[c].wait()
        extra = residual[:, columns(c)].astype(f32)
        mine = lax.div(lax.broadcasted_iota(jnp.int32, (BLOCK, SIZES[c]), 0), 8) == half
        extra = jnp.where(mine, jnp.concatenate([extra, extra], axis=0), 0.0)
        terms[own, columns(c)] = (terms[own, columns(c)].astype(f32) + extra).astype(bf16)

    sent, stores = [], []

    def send(src, dst, send_sem, recv_sem, there):
        copy = pltpu.make_async_remote_copy(
            src_ref=src, dst_ref=dst, send_sem=send_sem, recv_sem=recv_sem,
            device_id=there, device_id_type=MESH,
        )
        copy.start()
        sent.append(copy)

    def receive(dst, recv_sem):
        pltpu.make_async_remote_copy(
            src_ref=dst, dst_ref=dst, send_sem=recv_sem, recv_sem=recv_sem,
            device_id=(section, neighbour[0]), device_id_type=MESH,
        ).wait_recv()

    def reduce(c, s):
        for direction in range(2):
            length = hops(direction, c)
            if s > length:
                continue
            d = rows(offset(direction, length + 1 - s))
            if s == 1:
                src = terms.at[d, columns(c)]
            else:
                src = arrived.at[direction, s - 2, :, columns(c)]
                receive(src, reduce_recv.at[direction, s - 2, c])
                src[...] = (src[...].astype(f32) + terms[d, columns(c)].astype(f32)).astype(bf16)
            send(
                src,
                arrived.at[direction, s - 1, :, columns(c)],
                reduce_send.at[direction, s - 1, c],
                reduce_recv.at[direction, s - 1, c],
                (section, neighbour[direction]),
            )

    def finish(c, s):
        value = terms[rows(y), columns(c)].astype(f32)
        for direction in (1, 0) if hops(0, c) == 4 else (0, 1):
            last = hops(direction, c) - 1
            src = arrived.at[direction, last, :, columns(c)]
            receive(src, reduce_recv.at[direction, last, c])
            value = value + src[...].astype(f32)
        partial[:, columns(c)] = value.astype(bf16)
        def across(dst, recv_sem, there):
            return pltpu.make_async_remote_copy(
                src_ref=partial.at[:, columns(c)], dst_ref=dst, send_sem=cross_send.at[1, c], recv_sem=recv_sem,
                device_id=there, device_id_type=MESH,
            )

        direct = across(crossed.at[1, :, columns(c)], cross_recv.at[1, c], (after, far))
        if c in RELAYED:
            pl.when(by_relay)(across(relayed.at[:, columns(c)], relay_recv.at[c], relay_at).start)
            pl.when(jnp.logical_not(by_relay))(direct.start)
        else:
            direct.start()
        sent.append(direct)
        send(
            partial.at[:, columns(c)], crossed.at[0, :, columns(c)], cross_send.at[0, c], cross_recv.at[0, c],
            (after, t),
        )

    def passing(c):
        return pltpu.make_async_remote_copy(
            src_ref=relayed.at[:, columns(c)], dst_ref=crossed.at[1, :, columns(c)],
            send_sem=relay_send.at[c], recv_sem=cross_recv.at[1, c],
            device_id=relay_target, device_id_type=MESH,
        )

    def relay(c, s):
        @pl.when(is_relay)
        def _():
            receive(relayed.at[:, columns(c)], relay_recv.at[c])
            passing(c).start()

    def pass_on(c, s, d):
        for direction in range(2):
            if s > hops(direction, c):
                continue
            block = gathered.at[rows(offset(direction, -(s - 1))), columns(c)]
            if s > 1:
                receive(block, gather_recv.at[direction, s - 2, c])
            send(
                block, block, gather_send.at[direction, s - 1, c], gather_recv.at[direction, s - 1, c],
                (section, neighbour[direction]),
            )

    def hidden(c, s):
        for slot in range(2):
            receive(crossed.at[slot, :, columns(c)], cross_recv.at[slot, c])
        value = crossed[0, :, columns(c)].astype(f32) + crossed[1, :, columns(c)].astype(f32)
        gathered[rows(y), columns(c)] = value.astype(bf16)
        pass_on(c, 1, None)

    def gather(c, s):
        pass_on(c, s + 1, None)

    def product(c, s):
        for direction in range(2):
            last = hops(direction, c)
            block = gathered.at[rows(offset(direction, -last)), columns(c)]
            receive(block, gather_recv.at[direction, last - 1, c])
        piece = 256
        for j in range(SIZES[c] // piece):
            at = pl.ds(starts[c] + j * piece, piece)
            values = gathered[:, at].astype(f32)
            square = values * values
            square = square[:, :128] + square[:, 128:]
            if c == first_product and j == 0:
                squares[...] = square
            else:
                squares[...] += square
            values = jnp.clip(values * gain[0:1, at].astype(f32), -LIMIT, LIMIT)
            scaled[:, pl.ds(j * piece, piece)] = values.astype(bf16)
        result = jnp.dot(scaled[:, : SIZES[c]], mixed[columns(c), :], preferred_element_type=f32)
        if c == first_product:
            total[...] = result
        else:
            total[...] += result
        block = gathered[own, columns(c)].astype(f32)
        taken[:, columns(c)] = jnp.where(half == 0, block[:8], block[8:]).astype(bf16)
        stores.append(pltpu.make_async_copy(taken.at[:, columns(c)], stream.at[:, columns(c)], store_sem.at[c]))
        stores[-1].start()

    def mix(c, s):
        tiles = SIZES[c] // QTILE

        def one(i, carry):
            tile = starts[c] // QTILE + i
            at = pl.ds(pl.multiple_of(tile * QTILE, QTILE), QTILE)
            values = weight[at, :].astype(f32)
            result = None
            for b, bits in enumerate(BITS):
                power, low = powers[b, 0, 0, tile], LOWEST[b]
                step = jnp.where(power == low, 2.0**low, jnp.where(power == low + 1, 2.0 ** (low + 1), 2.0 ** (low + 2)))
                inverse = jnp.where(power == low, 2.0**-low, jnp.where(power == low + 1, 2.0 ** (-low - 1), 2.0 ** (-low - 2)))
                levels = jnp.clip(jnp.floor(values * inverse + 0.5), -(2.0 ** (bits - 1)), 2.0 ** (bits - 1) - 1.0)
                part = levels * (shares[b] * step)
                result = part if result is None else result + part
            mixed[at, :] = result.astype(bf16)
            return carry

        lax.fori_loop(0, tiles, one, 0)

    join(0, 0)
    pl.semaphore_wait(barrier, 5 - lax.rem(place, 2))
    reduce(0, 1)
    for c in range(1, CHUNKS):
        join(c, 0)
        if c < FIRST:
            reduce(c, 1)
    for load in loads[1:]:
        load.wait()
    first = jnp.int32(0)
    for q in range(sections):
        first = first + jnp.where(q < section, counts[q], 0)
    raised = [jnp.exp(jnp.full((8, 128), logits[b, first], f32)) for b in range(3)]
    whole = raised[0] + raised[1] + raised[2]
    shares = [(r / whole)[0:1, :] for r in raised]

    order = [x for x in schedule(CHUNKS) if x[0] != "reduce" or x[2] > 1 or x[1] >= FIRST]
    first_product = [c for name, c, s in order if name == "product"][0]
    act = dict(reduce=reduce, finish=finish, hidden=hidden, relay=relay, gather=gather, product=product, mix=mix)
    for name, c, s in order:
        act[name](c, s)

    mean = jnp.sum(squares[...], axis=1, keepdims=True) * (1.0 / depth)
    product_out[...] = (total[...] * lax.rsqrt(mean + 1e-05)).astype(bf16)
    stores.append(pltpu.make_async_copy(product_out, key_values, store_sem.at[CHUNKS]))
    stores[-1].start()
    for copy in sent:
        copy.wait_send()
    for copy in stores:
        copy.wait()

    @pl.when(is_relay)
    def _():
        for c in RELAYED:
            passing(c).wait_send()


def hand_out(stream_in, product_in, stream, key_values):
    stream[...] = stream_in[...]
    key_values[...] = product_in[...]


def body(down_terms, residual, norm_gain, key_value_weight, step_powers, bit_logits, layer_counts):
    terms, weight = down_terms[0], key_value_weight[0]
    depth, wide = weight.shape
    bf16, f32 = jnp.bfloat16, jnp.float32
    vmem, smem, anywhere = pltpu.VMEM, pltpu.SMEM, pl.ANY
    dma = pltpu.SemaphoreType.DMA
    out_shape = (
        jax.ShapeDtypeStruct(residual.shape, bf16),
        jax.ShapeDtypeStruct((terms.shape[0], wide), bf16),
    )
    powers = jnp.swapaxes(step_powers, 2, 3)
    logits = bit_logits.T
    outs = pl.pallas_call(
        kernel,
        out_shape=out_shape,
        in_specs=[pl.BlockSpec(memory_space=anywhere)] * 7,
        out_specs=(pl.BlockSpec(memory_space=anywhere),) * 2,
        scratch_shapes=[
            smem(powers.shape, jnp.int32),
            smem(logits.shape, f32),
            smem(layer_counts.shape, jnp.int32),
            vmem(norm_gain.shape, bf16),
            vmem(residual.shape, bf16),
            vmem((terms.shape[0], wide), bf16),
            vmem(terms.shape, bf16),
            vmem(residual.shape, bf16),
            vmem(weight.shape, bf16),
            vmem(weight.shape, bf16),
            vmem((2, 4, BLOCK, depth), bf16),
            vmem((BLOCK, depth), bf16),
            vmem((2, BLOCK, depth), bf16),
            vmem(terms.shape, bf16),
            vmem((terms.shape[0], max(SIZES)), bf16),
            vmem((terms.shape[0], wide), f32),
            vmem((terms.shape[0], 128), f32),
            dma((6,)),
            dma((CHUNKS,)),
            dma((CHUNKS + 1,)),
            dma((2, 4, CHUNKS)),
            dma((2, 4, CHUNKS)),
            dma((2, CHUNKS)),
            dma((2, CHUNKS)),
            dma((2, 4, CHUNKS)),
            dma((2, 4, CHUNKS)),
            vmem((BLOCK, depth), bf16),
            dma((CHUNKS,)),
            dma((CHUNKS,)),
        ],
        compiler_params=pltpu.CompilerParams(
            collective_id=0, has_side_effects=True, vmem_limit_bytes=56 << 20
        ),
    )(powers, logits, layer_counts, terms, residual, norm_gain, weight)
    return pl.pallas_call(
        hand_out,
        out_shape=out_shape,
        in_specs=[pl.BlockSpec(memory_space=vmem)] * 2,
        out_specs=(pl.BlockSpec(memory_space=vmem),) * 2,
        compiler_params=pltpu.CompilerParams(vmem_limit_bytes=56 << 20),
    )(*outs)


def solution(mesh):
    return jax.shard_map(
        body,
        mesh=mesh,
        in_specs=(
            P("tensor", "segment", None),
            P(("segment", "tensor"), None),
            P("segment", None),
            P("segment", None, "tensor"),
            P(None, "segment", None, "tensor"),
            P(),
            P(),
        ),
        out_specs=(P(("segment", "tensor"), None), P("segment", "tensor")),
        check_vma=False,
    )
```

```python
import jax
import jax.numpy as jnp
from jax import lax
from jax.experimental import pallas as pl
from jax.experimental.pallas import tpu as pltpu
from jax.sharding import PartitionSpec as P

MESH = pl.DeviceIdType.MESH
QTILE = 128
RING = 8
SIZES = (2048,) * 4
CHUNKS = len(SIZES)
STAGGER, STEP, CROSS, SPREAD = 0.75, 1.0, 4.0, 0.6
BLOCK = 16
LIMIT = 1e30
RELAY = 1.6
FIRST = 3
RELAYED = (0,)
RUN = 12
BITS = (2, 4, 8)
LOWEST = (-8, -9, -12)


def hops(direction, chunk):
    return 4 if (chunk + direction) % 2 == 0 else 3


def schedule(chunks, stagger=STAGGER, step=STEP, cross=CROSS):
    steps = []
    for c in range(chunks):
        begin = stagger * c
        for s in range(1, 5):
            steps.append((begin + step * (s - 1), 0, ("reduce", c, s)))
        done = begin + step * 4
        ready = step * 4 + cross + SPREAD * c
        steps.append((done, 0, ("finish", c, 0)))
        steps.append((ready, 1, ("hidden", c, 0)))
        if c in RELAYED:
            steps.append((done + RELAY, 0, ("relay", c, 0)))
        for s in range(1, 4):
            steps.append((ready + step * s, 1, ("gather", c, s)))
        steps.append((ready + step * 4.5, 2, ("product", c, 0)))
        steps.append((1.5 + 0.7 * c, 3, ("mix", c, 0)))
    steps.sort(key=lambda item: item[:2])
    return [item[2] for item in steps]


def kernel(
    powers_hbm, logits_hbm, counts_hbm, terms_hbm, residual_hbm, gain_hbm, weight_hbm,
    stream, key_values,
    powers, logits, counts, gain, taken, product_out,
    terms, residual, weight, mixed, arrived, partial, crossed, gathered, scaled, total, squares,
    load_sem, term_sem, store_sem, reduce_send, reduce_recv, cross_send, cross_recv, gather_send, gather_recv,
    relayed, relay_send, relay_recv,
):
    f32, bf16 = jnp.float32, jnp.bfloat16
    section, sections = lax.axis_index("segment"), lax.axis_size("segment")
    t = lax.axis_index("tensor")
    y, z = lax.rem(t, RING), lax.div(t, RING)
    ring = z * RING
    neighbour = (ring + lax.rem(y + 1, RING), ring + lax.rem(y + RING - 1, RING))
    far = lax.rem(t + RING, 2 * RING)
    after, before = lax.rem(section + 1, sections), lax.rem(section + sections - 1, sections)
    place = lax.rem(section, RUN)
    spot = lax.div(place, 2)
    first_core = lax.rem(place, 2) == 0
    by_relay = jnp.logical_and(lax.rem(spot, 2) == 1, first_core)
    is_relay = jnp.logical_and(lax.rem(spot, 2) == 0, first_core)
    last_spot = RUN // 2 - 1
    wrapped = lax.div(spot, last_spot)
    relay_at = (section - place + lax.rem(place + 2, RUN), lax.rem(t + RING * wrapped, 2 * RING))
    wraps = lax.div(last_spot - spot, last_spot)
    relay_source = (section - place + lax.rem(place + RUN - 2, RUN), lax.rem(t + RING * wraps, 2 * RING))
    relay_target = (section - place + lax.rem(place + RUN - 1, RUN), lax.rem(t + RING + RING * wraps, 2 * RING))
    is_target = jnp.logical_and(lax.rem(spot, 2) == 1, lax.rem(place, 2) == 1)
    relay_from = (section - place + lax.rem(place + 1, RUN), lax.rem(t + RING + RING * wrapped, 2 * RING))

    depth = terms.shape[1]
    starts = [sum(SIZES[:c]) for c in range(CHUNKS)]

    def columns(c):
        return pl.ds(starts[c], SIZES[c])

    def rows(d):
        return pl.ds(pl.multiple_of(lax.rem(d + 2 * RING, RING) * BLOCK, BLOCK), BLOCK)

    def offset(direction, distance):
        return y + distance if direction == 0 else y - distance

    barrier = pltpu.get_barrier_semaphore()
    for there in (neighbour[0], neighbour[1]):
        pl.semaphore_signal(barrier, inc=1, device_id=(section, there), device_id_type=MESH)
    for there in (t, far):
        pl.semaphore_signal(barrier, inc=1, device_id=(before, there), device_id_type=MESH)

    @pl.when(is_relay)
    def _():
        pl.semaphore_signal(barrier, inc=1, device_id=relay_source, device_id_type=MESH)

    @pl.when(is_target)
    def _():
        pl.semaphore_signal(barrier, inc=1, device_id=relay_from, device_id_type=MESH)

    loads = [
        pltpu.make_async_copy(src, dst, load_sem.at[i])
        for i, (src, dst) in enumerate((
            (residual_hbm, residual), (counts_hbm, counts), (logits_hbm, logits),
            (powers_hbm, powers), (weight_hbm, weight), (gain_hbm, gain),
        ))
    ]
    term_loads = [
        pltpu.make_async_copy(terms_hbm.at[:, columns(c)], terms.at[:, columns(c)], term_sem.at[c])
        for c in range(CHUNKS)
    ]
    loads[0].start()
    for load in term_loads + loads[1:]:
        load.start()

    loads[0].wait()
    own = pl.ds(pl.multiple_of(lax.div(t, 2) * BLOCK, BLOCK), BLOCK)
    half = lax.rem(t, 2)

    def join(c, s):
        term_loads[c].wait()
        extra = residual[:, columns(c)].astype(f32)
        mine = lax.div(lax.broadcasted_iota(jnp.int32, (BLOCK, SIZES[c]), 0), 8) == half
        extra = jnp.where(mine, jnp.concatenate([extra, extra], axis=0), 0.0)
        terms[own, columns(c)] = (terms[own, columns(c)].astype(f32) + extra).astype(bf16)

    sent, stores = [], []

    def send(src, dst, send_sem, recv_sem, there):
        copy = pltpu.make_async_remote_copy(
            src_ref=src, dst_ref=dst, send_sem=send_sem, recv_sem=recv_sem,
            device_id=there, device_id_type=MESH,
        )
        copy.start()
        sent.append(copy)

    def receive(dst, recv_sem):
        pltpu.make_async_remote_copy(
            src_ref=dst, dst_ref=dst, send_sem=recv_sem, recv_sem=recv_sem,
            device_id=(section, neighbour[0]), device_id_type=MESH,
        ).wait_recv()

    def reduce(c, s):
        for direction in range(2):
            length = hops(direction, c)
            if s > length:
                continue
            d = rows(offset(direction, length + 1 - s))
            if s == 1:
                src = terms.at[d, columns(c)]
            else:
                src = arrived.at[direction, s - 2, :, columns(c)]
                receive(src, reduce_recv.at[direction, s - 2, c])
                src[...] = (src[...].astype(f32) + terms[d, columns(c)].astype(f32)).astype(bf16)
            send(
                src,
                arrived.at[direction, s - 1, :, columns(c)],
                reduce_send.at[direction, s - 1, c],
                reduce_recv.at[direction, s - 1, c],
                (section, neighbour[direction]),
            )

    def finish(c, s):
        value = terms[rows(y), columns(c)].astype(f32)
        for direction in (1, 0) if hops(0, c) == 4 else (0, 1):
            last = hops(direction, c) - 1
            src = arrived.at[direction, last, :, columns(c)]
            receive(src, reduce_recv.at[direction, last, c])
            value = value + src[...].astype(f32)
        partial[:, columns(c)] = value.astype(bf16)
        def across(dst, recv_sem, there):
            return pltpu.make_async_remote_copy(
                src_ref=partial.at[:, columns(c)], dst_ref=dst, send_sem=cross_send.at[1, c], recv_sem=recv_sem,
                device_id=there, device_id_type=MESH,
            )

        direct = across(crossed.at[1, :, columns(c)], cross_recv.at[1, c], (after, far))
        if c in RELAYED:
            pl.when(by_relay)(across(relayed.at[:, columns(c)], relay_recv.at[c], relay_at).start)
            pl.when(jnp.logical_not(by_relay))(direct.start)
        else:
            direct.start()
        sent.append(direct)
        send(
            partial.at[:, columns(c)], crossed.at[0, :, columns(c)], cross_send.at[0, c], cross_recv.at[0, c],
            (after, t),
        )

    def passing(c):
        return pltpu.make_async_remote_copy(
            src_ref=relayed.at[:, columns(c)], dst_ref=crossed.at[1, :, columns(c)],
            send_sem=relay_send.at[c], recv_sem=cross_recv.at[1, c],
            device_id=relay_target, device_id_type=MESH,
        )

    def relay(c, s):
        @pl.when(is_relay)
        def _():
            receive(relayed.at[:, columns(c)], relay_recv.at[c])
            passing(c).start()

    def pass_on(c, s, d):
        for direction in range(2):
            if s > hops(direction, c):
                continue
            block = gathered.at[rows(offset(direction, -(s - 1))), columns(c)]
            if s > 1:
                receive(block, gather_recv.at[direction, s - 2, c])
            send(
                block, block, gather_send.at[direction, s - 1, c], gather_recv.at[direction, s - 1, c],
                (section, neighbour[direction]),
            )

    def hidden(c, s):
        for slot in range(2):
            receive(crossed.at[slot, :, columns(c)], cross_recv.at[slot, c])
        value = crossed[0, :, columns(c)].astype(f32) + crossed[1, :, columns(c)].astype(f32)
        gathered[rows(y), columns(c)] = value.astype(bf16)
        pass_on(c, 1, None)

    def gather(c, s):
        pass_on(c, s + 1, None)

    def product(c, s):
        for direction in range(2):
            last = hops(direction, c)
            block = gathered.at[rows(offset(direction, -last)), columns(c)]
            receive(block, gather_recv.at[direction, last - 1, c])
        piece = 256
        for j in range(SIZES[c] // piece):
            at = pl.ds(starts[c] + j * piece, piece)
            values = gathered[:, at].astype(f32)
            square = values * values
            square = square[:, :128] + square[:, 128:]
            if c == first_product and j == 0:
                squares[...] = square
            else:
                squares[...] += square
            values = jnp.clip(values * gain[0:1, at].astype(f32), -LIMIT, LIMIT)
            scaled[:, pl.ds(j * piece, piece)] = values.astype(bf16)
        result = jnp.dot(scaled[:, : SIZES[c]], mixed[columns(c), :], preferred_element_type=f32)
        if c == first_product:
            total[...] = result
        else:
            total[...] += result
        block = gathered[own, columns(c)].astype(f32)
        taken[:, columns(c)] = jnp.where(half == 0, block[:8], block[8:]).astype(bf16)
        stores.append(pltpu.make_async_copy(taken.at[:, columns(c)], stream.at[:, columns(c)], store_sem.at[c]))
        stores[-1].start()

    def mix(c, s):
        tiles = SIZES[c] // QTILE

        def one(i, carry):
            tile = starts[c] // QTILE + i
            at = pl.ds(pl.multiple_of(tile * QTILE, QTILE), QTILE)
            values = weight[at, :].astype(f32)
            result = None
            for b, bits in enumerate(BITS):
                power, low = powers[b, 0, 0, tile], LOWEST[b]
                step = jnp.where(power == low, 2.0**low, jnp.where(power == low + 1, 2.0 ** (low + 1), 2.0 ** (low + 2)))
                inverse = jnp.where(power == low, 2.0**-low, jnp.where(power == low + 1, 2.0 ** (-low - 1), 2.0 ** (-low - 2)))
                levels = jnp.clip(jnp.floor(values * inverse + 0.5), -(2.0 ** (bits - 1)), 2.0 ** (bits - 1) - 1.0)
                part = levels * (shares[b] * step)
                result = part if result is None else result + part
            mixed[at, :] = result.astype(bf16)
            return carry

        lax.fori_loop(0, tiles, one, 0)

    join(0, 0)
    pl.semaphore_wait(barrier, 5 - lax.rem(place, 2))
    reduce(0, 1)
    for c in range(1, CHUNKS):
        join(c, 0)
        if c < FIRST:
            reduce(c, 1)
    for load in loads[1:]:
        load.wait()
    first = jnp.int32(0)
    for q in range(sections):
        first = first + jnp.where(q < section, counts[q], 0)
    raised = [jnp.exp(jnp.full((8, 128), logits[b, first], f32)) for b in range(3)]
    whole = raised[0] + raised[1] + raised[2]
    shares = [(r / whole)[0:1, :] for r in raised]

    order = [x for x in schedule(CHUNKS) if x[0] != "reduce" or x[2] > 1 or x[1] >= FIRST]
    first_product = [c for name, c, s in order if name == "product"][0]
    act = dict(reduce=reduce, finish=finish, hidden=hidden, relay=relay, gather=gather, product=product, mix=mix)
    for name, c, s in order:
        act[name](c, s)

    mean = jnp.sum(squares[...], axis=1, keepdims=True) * (1.0 / depth)
    product_out[...] = (total[...] * lax.rsqrt(mean + 1e-05)).astype(bf16)
    stores.append(pltpu.make_async_copy(product_out, key_values, store_sem.at[CHUNKS]))
    stores[-1].start()
    for copy in sent:
        copy.wait_send()
    for copy in stores:
        copy.wait()

    @pl.when(is_relay)
    def _():
        for c in RELAYED:
            passing(c).wait_send()


def hand_out(stream_in, product_in, stream, key_values):
    stream[...] = stream_in[...]
    key_values[...] = product_in[...]


def body(down_terms, residual, norm_gain, key_value_weight, step_powers, bit_logits, layer_counts):
    terms, weight = down_terms[0], key_value_weight[0]
    depth, wide = weight.shape
    bf16, f32 = jnp.bfloat16, jnp.float32
    vmem, smem, anywhere = pltpu.VMEM, pltpu.SMEM, pl.ANY
    dma = pltpu.SemaphoreType.DMA
    out_shape = (
        jax.ShapeDtypeStruct(residual.shape, bf16),
        jax.ShapeDtypeStruct((terms.shape[0], wide), bf16),
    )
    powers = jnp.swapaxes(step_powers, 2, 3)
    logits = bit_logits.T
    outs = pl.pallas_call(
        kernel,
        out_shape=out_shape,
        in_specs=[pl.BlockSpec(memory_space=anywhere)] * 7,
        out_specs=(pl.BlockSpec(memory_space=anywhere),) * 2,
        scratch_shapes=[
            smem(powers.shape, jnp.int32),
            smem(logits.shape, f32),
            smem(layer_counts.shape, jnp.int32),
            vmem(norm_gain.shape, bf16),
            vmem(residual.shape, bf16),
            vmem((terms.shape[0], wide), bf16),
            vmem(terms.shape, bf16),
            vmem(residual.shape, bf16),
            vmem(weight.shape, bf16),
            vmem(weight.shape, bf16),
            vmem((2, 4, BLOCK, depth), bf16),
            vmem((BLOCK, depth), bf16),
            vmem((2, BLOCK, depth), bf16),
            vmem(terms.shape, bf16),
            vmem((terms.shape[0], max(SIZES)), bf16),
            vmem((terms.shape[0], wide), f32),
            vmem((terms.shape[0], 128), f32),
            dma((6,)),
            dma((CHUNKS,)),
            dma((CHUNKS + 1,)),
            dma((2, 4, CHUNKS)),
            dma((2, 4, CHUNKS)),
            dma((2, CHUNKS)),
            dma((2, CHUNKS)),
            dma((2, 4, CHUNKS)),
            dma((2, 4, CHUNKS)),
            vmem((BLOCK, depth), bf16),
            dma((CHUNKS,)),
            dma((CHUNKS,)),
        ],
        compiler_params=pltpu.CompilerParams(
            collective_id=0, has_side_effects=True, vmem_limit_bytes=56 << 20
        ),
    )(powers, logits, layer_counts, terms, residual, norm_gain, weight)
    return pl.pallas_call(
        hand_out,
        out_shape=out_shape,
        in_specs=[pl.BlockSpec(memory_space=vmem)] * 2,
        out_specs=(pl.BlockSpec(memory_space=vmem),) * 2,
        compiler_params=pltpu.CompilerParams(vmem_limit_bytes=56 << 20),
    )(*outs)


def solution(mesh):
    return jax.shard_map(
        body,
        mesh=mesh,
        in_specs=(
            P("tensor", "segment", None),
            P(("segment", "tensor"), None),
            P("segment", None),
            P("segment", None, "tensor"),
            P(None, "segment", None, "tensor"),
            P(),
            P(),
        ),
        out_specs=(P(("segment", "tensor"), None), P("segment", "tensor")),
        check_vma=False,
    )
```

```python
import jax
import jax.numpy as jnp
from jax import lax
from jax.experimental import pallas as pl
from jax.experimental.pallas import tpu as pltpu
from jax.sharding import PartitionSpec as P

MESH = pl.DeviceIdType.MESH
QTILE = 128
RING = 8
SIZES = (2048,) * 4
CHUNKS = len(SIZES)
STAGGER, STEP, CROSS, SPREAD = 0.75, 1.0, 4.0, 0.6
BLOCK = 16
LIMIT = 1e30
RELAY = 1.6
FIRST = 3
RELAYED = (0,)
RUN = 12
BITS = (2, 4, 8)
LOWEST = (-8, -9, -12)


def hops(direction, chunk):
    return 4 if (chunk + direction) % 2 == 0 else 3


def schedule(chunks, stagger=STAGGER, step=STEP, cross=CROSS):
    steps = []
    for c in range(chunks):
        begin = stagger * c
        for s in range(1, 5):
            steps.append((begin + step * (s - 1), 0, ("reduce", c, s)))
        done = begin + step * 4
        ready = step * 4 + cross + SPREAD * c
        steps.append((done, 0, ("finish", c, 0)))
        steps.append((ready, 1, ("hidden", c, 0)))
        if c in RELAYED:
            steps.append((done + RELAY, 0, ("relay", c, 0)))
        for s in range(1, 4):
            steps.append((ready + step * s, 1, ("gather", c, s)))
        steps.append((ready + step * 4.9, 2, ("product", c, 0)))
        steps.append((1.5 + 0.7 * c, 3, ("mix", c, 0)))
    steps.sort(key=lambda item: item[:2])
    return [item[2] for item in steps]


def kernel(
    powers_hbm, logits_hbm, counts_hbm, terms_hbm, residual_hbm, gain_hbm, weight_hbm,
    stream, key_values,
    powers, logits, counts, gain, taken, product_out,
    terms, residual, weight, mixed, arrived, partial, crossed, gathered, scaled, total, squares,
    load_sem, term_sem, store_sem, reduce_send, reduce_recv, cross_send, cross_recv, gather_send, gather_recv,
    relayed, relay_send, relay_recv,
):
    f32, bf16 = jnp.float32, jnp.bfloat16
    section, sections = lax.axis_index("segment"), lax.axis_size("segment")
    t = lax.axis_index("tensor")
    y, z = lax.rem(t, RING), lax.div(t, RING)
    ring = z * RING
    neighbour = (ring + lax.rem(y + 1, RING), ring + lax.rem(y + RING - 1, RING))
    far = lax.rem(t + RING, 2 * RING)
    after, before = lax.rem(section + 1, sections), lax.rem(section + sections - 1, sections)
    place = lax.rem(section, RUN)
    spot = lax.div(place, 2)
    first_core = lax.rem(place, 2) == 0
    by_relay = jnp.logical_and(lax.rem(spot, 2) == 1, first_core)
    is_relay = jnp.logical_and(lax.rem(spot, 2) == 0, first_core)
    last_spot = RUN // 2 - 1
    wrapped = lax.div(spot, last_spot)
    relay_at = (section - place + lax.rem(place + 2, RUN), lax.rem(t + RING * wrapped, 2 * RING))
    wraps = lax.div(last_spot - spot, last_spot)
    relay_source = (section - place + lax.rem(place + RUN - 2, RUN), lax.rem(t + RING * wraps, 2 * RING))
    relay_target = (section - place + lax.rem(place + RUN - 1, RUN), lax.rem(t + RING + RING * wraps, 2 * RING))
    is_target = jnp.logical_and(lax.rem(spot, 2) == 1, lax.rem(place, 2) == 1)
    relay_from = (section - place + lax.rem(place + 1, RUN), lax.rem(t + RING + RING * wrapped, 2 * RING))

    depth = terms.shape[1]
    starts = [sum(SIZES[:c]) for c in range(CHUNKS)]

    def columns(c):
        return pl.ds(starts[c], SIZES[c])

    def rows(d):
        return pl.ds(pl.multiple_of(lax.rem(d + 2 * RING, RING) * BLOCK, BLOCK), BLOCK)

    def offset(direction, distance):
        return y + distance if direction == 0 else y - distance

    barrier = pltpu.get_barrier_semaphore()
    for there in (neighbour[0], neighbour[1]):
        pl.semaphore_signal(barrier, inc=1, device_id=(section, there), device_id_type=MESH)
    for there in (t, far):
        pl.semaphore_signal(barrier, inc=1, device_id=(before, there), device_id_type=MESH)

    @pl.when(is_relay)
    def _():
        pl.semaphore_signal(barrier, inc=1, device_id=relay_source, device_id_type=MESH)

    @pl.when(is_target)
    def _():
        pl.semaphore_signal(barrier, inc=1, device_id=relay_from, device_id_type=MESH)

    loads = [
        pltpu.make_async_copy(src, dst, load_sem.at[i])
        for i, (src, dst) in enumerate((
            (residual_hbm, residual), (counts_hbm, counts), (logits_hbm, logits),
            (powers_hbm, powers), (weight_hbm, weight), (gain_hbm, gain),
        ))
    ]
    term_loads = [
        pltpu.make_async_copy(terms_hbm.at[:, columns(c)], terms.at[:, columns(c)], term_sem.at[c])
        for c in range(CHUNKS)
    ]
    loads[0].start()
    for load in term_loads + loads[1:]:
        load.start()

    loads[0].wait()
    own = pl.ds(pl.multiple_of(lax.div(t, 2) * BLOCK, BLOCK), BLOCK)
    half = lax.rem(t, 2)

    def join(c, s):
        term_loads[c].wait()
        extra = residual[:, columns(c)].astype(f32)
        mine = lax.div(lax.broadcasted_iota(jnp.int32, (BLOCK, SIZES[c]), 0), 8) == half
        extra = jnp.where(mine, jnp.concatenate([extra, extra], axis=0), 0.0)
        terms[own, columns(c)] = (terms[own, columns(c)].astype(f32) + extra).astype(bf16)

    sent, stores = [], []

    def send(src, dst, send_sem, recv_sem, there):
        copy = pltpu.make_async_remote_copy(
            src_ref=src, dst_ref=dst, send_sem=send_sem, recv_sem=recv_sem,
            device_id=there, device_id_type=MESH,
        )
        copy.start()
        sent.append(copy)

    def receive(dst, recv_sem):
        pltpu.make_async_remote_copy(
            src_ref=dst, dst_ref=dst, send_sem=recv_sem, recv_sem=recv_sem,
            device_id=(section, neighbour[0]), device_id_type=MESH,
        ).wait_recv()

    def reduce(c, s):
        for direction in range(2):
            length = hops(direction, c)
            if s > length:
                continue
            d = rows(offset(direction, length + 1 - s))
            if s == 1:
                src = terms.at[d, columns(c)]
            else:
                src = arrived.at[direction, s - 2, :, columns(c)]
                receive(src, reduce_recv.at[direction, s - 2, c])
                src[...] = (src[...].astype(f32) + terms[d, columns(c)].astype(f32)).astype(bf16)
            send(
                src,
                arrived.at[direction, s - 1, :, columns(c)],
                reduce_send.at[direction, s - 1, c],
                reduce_recv.at[direction, s - 1, c],
                (section, neighbour[direction]),
            )

    def finish(c, s):
        value = terms[rows(y), columns(c)].astype(f32)
        for direction in (1, 0) if hops(0, c) == 4 else (0, 1):
            last = hops(direction, c) - 1
            src = arrived.at[direction, last, :, columns(c)]
            receive(src, reduce_recv.at[direction, last, c])
            value = value + src[...].astype(f32)
        partial[:, columns(c)] = value.astype(bf16)
        def across(dst, recv_sem, there):
            return pltpu.make_async_remote_copy(
                src_ref=partial.at[:, columns(c)], dst_ref=dst, send_sem=cross_send.at[1, c], recv_sem=recv_sem,
                device_id=there, device_id_type=MESH,
            )

        direct = across(crossed.at[1, :, columns(c)], cross_recv.at[1, c], (after, far))
        if c in RELAYED:
            pl.when(by_relay)(across(relayed.at[:, columns(c)], relay_recv.at[c], relay_at).start)
            pl.when(jnp.logical_not(by_relay))(direct.start)
        else:
            direct.start()
        sent.append(direct)
        send(
            partial.at[:, columns(c)], crossed.at[0, :, columns(c)], cross_send.at[0, c], cross_recv.at[0, c],
            (after, t),
        )

    def passing(c):
        return pltpu.make_async_remote_copy(
            src_ref=relayed.at[:, columns(c)], dst_ref=crossed.at[1, :, columns(c)],
            send_sem=relay_send.at[c], recv_sem=cross_recv.at[1, c],
            device_id=relay_target, device_id_type=MESH,
        )

    def relay(c, s):
        @pl.when(is_relay)
        def _():
            receive(relayed.at[:, columns(c)], relay_recv.at[c])
            passing(c).start()

    def pass_on(c, s, d):
        for direction in range(2):
            if s > hops(direction, c):
                continue
            block = gathered.at[rows(offset(direction, -(s - 1))), columns(c)]
            if s > 1:
                receive(block, gather_recv.at[direction, s - 2, c])
            send(
                block, block, gather_send.at[direction, s - 1, c], gather_recv.at[direction, s - 1, c],
                (section, neighbour[direction]),
            )

    def hidden(c, s):
        for slot in range(2):
            receive(crossed.at[slot, :, columns(c)], cross_recv.at[slot, c])
        value = crossed[0, :, columns(c)].astype(f32) + crossed[1, :, columns(c)].astype(f32)
        gathered[rows(y), columns(c)] = value.astype(bf16)
        pass_on(c, 1, None)

    def gather(c, s):
        pass_on(c, s + 1, None)

    def product(c, s):
        for direction in range(2):
            last = hops(direction, c)
            block = gathered.at[rows(offset(direction, -last)), columns(c)]
            receive(block, gather_recv.at[direction, last - 1, c])
        piece = 256
        for j in range(SIZES[c] // piece):
            at = pl.ds(starts[c] + j * piece, piece)
            values = gathered[:, at].astype(f32)
            square = values * values
            square = square[:, :128] + square[:, 128:]
            if c == first_product and j == 0:
                squares[...] = square
            else:
                squares[...] += square
            values = jnp.clip(values * gain[0:1, at].astype(f32), -LIMIT, LIMIT)
            scaled[:, pl.ds(j * piece, piece)] = values.astype(bf16)
        result = jnp.dot(scaled[:, : SIZES[c]], mixed[columns(c), :], preferred_element_type=f32)
        if c == first_product:
            total[...] = result
        else:
            total[...] += result
        block = gathered[own, columns(c)].astype(f32)
        taken[:, columns(c)] = jnp.where(half == 0, block[:8], block[8:]).astype(bf16)
        stores.append(pltpu.make_async_copy(taken.at[:, columns(c)], stream.at[:, columns(c)], store_sem.at[c]))
        stores[-1].start()

    def mix(c, s):
        tiles = SIZES[c] // QTILE

        def one(i, carry):
            tile = starts[c] // QTILE + i
            at = pl.ds(pl.multiple_of(tile * QTILE, QTILE), QTILE)
            values = weight[at, :].astype(f32)
            result = None
            for b, bits in enumerate(BITS):
                power, low = powers[b, 0, 0, tile], LOWEST[b]
                step = jnp.where(power == low, 2.0**low, jnp.where(power == low + 1, 2.0 ** (low + 1), 2.0 ** (low + 2)))
                inverse = jnp.where(power == low, 2.0**-low, jnp.where(power == low + 1, 2.0 ** (-low - 1), 2.0 ** (-low - 2)))
                levels = jnp.clip(jnp.floor(values * inverse + 0.5), -(2.0 ** (bits - 1)), 2.0 ** (bits - 1) - 1.0)
                part = levels * (shares[b] * step)
                result = part if result is None else result + part
            mixed[at, :] = result.astype(bf16)
            return carry

        lax.fori_loop(0, tiles, one, 0)

    join(0, 0)
    pl.semaphore_wait(barrier, 5 - lax.rem(place, 2))
    reduce(0, 1)
    for c in range(1, CHUNKS):
        join(c, 0)
        if c < FIRST:
            reduce(c, 1)
    for load in loads[1:]:
        load.wait()
    first = jnp.int32(0)
    for q in range(sections):
        first = first + jnp.where(q < section, counts[q], 0)
    raised = [jnp.exp(jnp.full((8, 128), logits[b, first], f32)) for b in range(3)]
    whole = raised[0] + raised[1] + raised[2]
    shares = [(r / whole)[0:1, :] for r in raised]

    order = [x for x in schedule(CHUNKS) if x[0] != "reduce" or x[2] > 1 or x[1] >= FIRST]
    first_product = [c for name, c, s in order if name == "product"][0]
    act = dict(reduce=reduce, finish=finish, hidden=hidden, relay=relay, gather=gather, product=product, mix=mix)
    for name, c, s in order:
        act[name](c, s)

    mean = jnp.sum(squares[...], axis=1, keepdims=True) * (1.0 / depth)
    product_out[...] = (total[...] * lax.rsqrt(mean + 1e-05)).astype(bf16)
    stores.append(pltpu.make_async_copy(product_out, key_values, store_sem.at[CHUNKS]))
    stores[-1].start()
    for copy in sent:
        copy.wait_send()
    for copy in stores:
        copy.wait()

    @pl.when(is_relay)
    def _():
        for c in RELAYED:
            passing(c).wait_send()


def hand_out(stream_in, product_in, stream, key_values):
    stream[...] = stream_in[...]
    key_values[...] = product_in[...]


def body(down_terms, residual, norm_gain, key_value_weight, step_powers, bit_logits, layer_counts):
    terms, weight = down_terms[0], key_value_weight[0]
    depth, wide = weight.shape
    bf16, f32 = jnp.bfloat16, jnp.float32
    vmem, smem, anywhere = pltpu.VMEM, pltpu.SMEM, pl.ANY
    dma = pltpu.SemaphoreType.DMA
    out_shape = (
        jax.ShapeDtypeStruct(residual.shape, bf16),
        jax.ShapeDtypeStruct((terms.shape[0], wide), bf16),
    )
    powers = jnp.swapaxes(step_powers, 2, 3)
    logits = bit_logits.T
    outs = pl.pallas_call(
        kernel,
        out_shape=out_shape,
        in_specs=[pl.BlockSpec(memory_space=anywhere)] * 7,
        out_specs=(pl.BlockSpec(memory_space=anywhere),) * 2,
        scratch_shapes=[
            smem(powers.shape, jnp.int32),
            smem(logits.shape, f32),
            smem(layer_counts.shape, jnp.int32),
            vmem(norm_gain.shape, bf16),
            vmem(residual.shape, bf16),
            vmem((terms.shape[0], wide), bf16),
            vmem(terms.shape, bf16),
            vmem(residual.shape, bf16),
            vmem(weight.shape, bf16),
            vmem(weight.shape, bf16),
            vmem((2, 4, BLOCK, depth), bf16),
            vmem((BLOCK, depth), bf16),
            vmem((2, BLOCK, depth), bf16),
            vmem(terms.shape, bf16),
            vmem((terms.shape[0], max(SIZES)), bf16),
            vmem((terms.shape[0], wide), f32),
            vmem((terms.shape[0], 128), f32),
            dma((6,)),
            dma((CHUNKS,)),
            dma((CHUNKS + 1,)),
            dma((2, 4, CHUNKS)),
            dma((2, 4, CHUNKS)),
            dma((2, CHUNKS)),
            dma((2, CHUNKS)),
            dma((2, 4, CHUNKS)),
            dma((2, 4, CHUNKS)),
            vmem((BLOCK, depth), bf16),
            dma((CHUNKS,)),
            dma((CHUNKS,)),
        ],
        compiler_params=pltpu.CompilerParams(
            collective_id=0, has_side_effects=True, vmem_limit_bytes=56 << 20
        ),
    )(powers, logits, layer_counts, terms, residual, norm_gain, weight)
    return pl.pallas_call(
        hand_out,
        out_shape=out_shape,
        in_specs=[pl.BlockSpec(memory_space=vmem)] * 2,
        out_specs=(pl.BlockSpec(memory_space=vmem),) * 2,
        compiler_params=pltpu.CompilerParams(vmem_limit_bytes=56 << 20),
    )(*outs)


def solution(mesh):
    return jax.shard_map(
        body,
        mesh=mesh,
        in_specs=(
            P("tensor", "segment", None),
            P(("segment", "tensor"), None),
            P("segment", None),
            P("segment", None, "tensor"),
            P(None, "segment", None, "tensor"),
            P(),
            P(),
        ),
        out_specs=(P(("segment", "tensor"), None), P("segment", "tensor")),
        check_vma=False,
    )
```
